256 devices in a mesh: grp: 8 (over z_hi, y), dev: 32 (over x, z_lo, core).
Axes of the slice: x: 4, y: 4, z: 8 (z_hi: 2, z_lo: 4; z = z_hi * 4 + z_lo), core: 2. Of those that a mesh axis runs over, the one named last changes fastest.
Arguments:
- embeddings: bfloat16 [98304, 768], P(('grp', 'dev')), may hold values from -6 to 6
- labels: bfloat16 [98304, 896], P(('grp', 'dev')), may hold values from -6 to 6
- cluster_rows: int32 [256], P(('grp', 'dev')), may hold values from 96 to 384, as said below
Outputs:
- propagated: bfloat16 [98304, 896], P(('grp', 'dev'))
The draws below stay inside these ranges and needn't reach their ends.
Inputs may be any that keep to these rules, and one draw needn't show every extreme that they name: `cluster_rows`: some cluster has all 384 slots filled and some has 96.
All inputs are finite; a program needn't handle non-finite values.
Results may differ from the reference program's by a relative error of at most 0.006.
Values may be sent and summed in bfloat16 or wider, within the bound.
A program may use at most 64 MiB of HBM per device.

```python
import math
import jax
import jax.numpy as jnp
from jax import lax

D = 768
C = 896
ROWS = 384
INNER = 4
GROUPS = 8
OWNERS = 32
CLUSTERS = 256
TOTAL_ROWS = 98304


def draw_cluster_rows(key, part):
    key = jax.random.fold_in(key, 11)
    first_key, second_key = jax.random.split(key)
    counts = jax.random.randint(first_key, (CLUSTERS,), ROWS // 4, ROWS + 1)
    order = jax.random.permutation(second_key, CLUSTERS)
    counts = counts.at[order[0]].set(ROWS)
    counts = counts.at[order[1]].set(ROWS // 4)
    return counts.astype(jnp.int32)


def shard_levels(stream_key, shape, cuts, smallest, largest):
    def one(dim, parts):
        draws = jax.random.uniform(jax.random.fold_in(jax.random.fold_in(stream_key, 6), dim), (parts,), jnp.float32, smallest / len(cuts), largest / len(cuts))
        return jnp.repeat(jnp.exp(draws), shape[dim] // parts).reshape((-1,) + (1,) * (len(shape) - dim - 1))

    level = one(*cuts[0])
    for cut in cuts[1:]:
        level = level * one(*cut)
    return level


def noise(key, shape, deviation, reach, pieces=(), held_as=jnp.bfloat16):
    drawn = deviation * jax.random.normal(key, shape, jnp.float32)
    if pieces:
        drawn = drawn * shard_levels(key, shape, pieces, -0.22, 0.18)
    return jnp.clip(drawn, -reach, reach).astype(held_as)


def setup_inputs(seed: int = 0) -> dict:
    splits = jax.random.split(jax.random.key(seed), 4)
    embeddings = noise(splits[0], (TOTAL_ROWS, D), 1.0, 6.0, ((0, 256),))
    labels = noise(splits[1], (TOTAL_ROWS, C), 1.0, 6.0, ((0, 256),))
    cluster_rows = draw_cluster_rows(jax.random.fold_in(splits[3], 71), 0)
    return dict(embeddings=embeddings, labels=labels, cluster_rows=cluster_rows)


sharpness = 25.0
keep_share = 0.8

def unit_rows(embeddings):
    values = embeddings.astype(jnp.float32)
    scaled = values * lax.rsqrt(lax.optimization_barrier(jnp.mean(values * values, axis=-1, keepdims=True)) + 1e-06)
    return (scaled / math.sqrt(values.shape[-1])).astype(jnp.bfloat16)

def raw_affinity(left_unit, right_unit):
    cosine = jnp.dot(left_unit, right_unit.T, preferred_element_type=jnp.float32)
    return jnp.exp(sharpness * cosine)

def reference(embeddings, labels, cluster_rows):
    label_shape = (GROUPS, OWNERS, ROWS, C)
    unit_vectors = unit_rows(embeddings).reshape(GROUPS, OWNERS, ROWS, D)
    places = lax.iota(jnp.int32, ROWS)
    row_valid = (places[None, :] < cluster_rows[:, None]).astype(jnp.float32).reshape(GROUPS, OWNERS, ROWS, 1)
    seed_labels = labels.reshape(label_shape) * row_valid.astype(jnp.bfloat16)
    offdiag = (places[:, None] != places[None, :]).astype(jnp.float32)

    def flatten(array):
        return array.reshape((CLUSTERS,) + array.shape[2:])

    def self_term(operands):
        left_unit, own_labels = operands
        pair_tile = (raw_affinity(left_unit, left_unit) * offdiag).astype(jnp.bfloat16)
        return jnp.dot(pair_tile, own_labels, preferred_element_type=jnp.float32)

    def pair_terms(operands):
        left_unit, right_unit, own_labels, far_labels = operands
        pair_tile = raw_affinity(left_unit, right_unit).astype(jnp.bfloat16)
        forward = jnp.dot(pair_tile, far_labels, preferred_element_type=jnp.float32)
        backward = jnp.dot(pair_tile.T, own_labels, preferred_element_type=jnp.float32)
        return (forward, backward)
    offsets = [(1, stride) for stride in range(1, INNER + 1)] + [(0, 1)]
    current = seed_labels
    for sweep_index in range(2):
        summed = lax.map(self_term, (flatten(unit_vectors), flatten(current))).reshape(label_shape)
        for axis_number, stride in offsets:
            right_unit = jnp.roll(unit_vectors, -stride, axis=axis_number)
            far_labels = jnp.roll(current, -stride, axis=axis_number)
            forward, backward = lax.map(pair_terms, (flatten(unit_vectors), flatten(right_unit), flatten(current), flatten(far_labels)))
            summed = summed + forward.reshape(label_shape)
            summed = summed + jnp.roll(backward.reshape(label_shape), stride, axis=axis_number)
        factor = lax.rsqrt(lax.optimization_barrier(jnp.mean(summed * summed, axis=-1, keepdims=True)) + 1e-06)
        mixed = keep_share * summed * factor + (1.0 - keep_share) * seed_labels.astype(jnp.float32)
        current = (mixed * row_valid).astype(jnp.bfloat16)
    return current.reshape(TOTAL_ROWS, C)
```

```python
import functools
import math

import jax
import jax.numpy as jnp
from jax import lax
from jax.experimental import pallas as pl
from jax.experimental.pallas import tpu as pltpu
from jax.sharding import PartitionSpec as P

MESH = pl.DeviceIdType.MESH
F32 = jnp.float32
BF16 = jnp.bfloat16

sharpness = 25.0
keep_share = 0.8

ROWS = 384
WIDTH = 768
CLASSES = 896
LANE = 128
UN = 6
UROWS = ROWS // UN
LN = CLASSES // LANE

OWN, OUTER, INNER2, OUTER2, INNER3, OUTER3, NEXT, PREV = range(8)
SLOTS = 8

(S_OWN, S_UP, S_DOWN, S_OUTER, S_INNER2, S_OUTER2, S_WRAP_I, S_WRAP_O, S_SIB_OWN, S_SIB_OUTER, S_PART0, S_PART1,
 S_SUM) = range(13)

T_OWN, T_SIB, T_OUT, T_OUTSIB = 0, 7, 11, 15
N_TILES = 18
OWN_SOURCES = (OWN, OUTER, INNER2, OUTER2, OUTER3, NEXT, PREV)
SIB_SOURCES = (OWN, OUTER, INNER2, None)
OUT_SOURCES = (OWN, INNER2, INNER3, OUTER3)
OUTSIB_SOURCES = (OWN, OUTER3, None)


def kernel(
    count_ref, emb_ref, lab_ref, out_ref,
    ubuf, lbuf, sibu, tiles, acc, acco, psend0, psend1, precv0, precv1, ssend, srecv,
    ssem, urecv, lrecv, sibrecv, prsem, srsem,
):
    g, d = lax.axis_index("grp"), lax.axis_index("dev")
    x, k, c = d // 8, (d // 2) % 4, d % 2
    z, y = (g // 4) * 4 + k, g % 4
    s = 1 - 2 * (k // 2)
    inner = (k == 1) | (k == 2)
    edge = (y == 0) | (y == 3)

    def at(x, y, z, c):
        x, y, z = (x + 4) % 4, (y + 4) % 4, (z + 16) % 8
        return ((z // 4) * 4 + y, x * 8 + (z % 4) * 2 + c)

    sibling = at(x, y, z, 1 - c)
    ahead = at(x, y, z + s, c)
    behind = at(x, y, z - s, c)
    up, down = at(x, y + 1, z, c), at(x, y - 1, z, c)
    right, left = at(x + s, y, z, c), at(x - s, y, z, c)
    wrap_i = at(x, 3 - y, z + s + 4, c)
    wrap_o = at(x, 3 - y, z + 2 * s + 4, c)
    wrap_slot = NEXT + y // 3
    relay = at(x, 3 - y, z + 4 + s * (2 - ((k == 1) | (k == 2)).astype(jnp.int32)), c)
    side = (c + k // 2) % 2
    sib_slot = OUTER2 + 2 * side
    outsib_slot = INNER2 + 2 * side

    barrier = pltpu.get_barrier_semaphore()

    def greet(device):
        pl.semaphore_signal(barrier, inc=1, device_id=device, device_id_type=MESH)

    for device in (sibling, ahead, behind, up, down, right, left):
        greet(device)

    @pl.when(edge)
    def _():
        greet(relay)

    @pl.when(edge & inner)
    def _():
        greet(wrap_i)
        greet(wrap_o)

    def copy(src, dst, send_sem, recv_sem, device):
        return pltpu.make_async_remote_copy(
            src_ref=src, dst_ref=dst, send_sem=send_sem, recv_sem=recv_sem, device_id=device,
            device_id_type=MESH,
        )

    def rows(slot, i):
        return ubuf.at[slot, pl.ds(pl.multiple_of(i * UROWS, UROWS), UROWS)]

    def send_u(src_slot, dst_slot, i, stream, device):
        copy(
            rows(src_slot, i), rows(dst_slot, i), ssem.at[stream, 0], urecv.at[dst_slot, i], device
        ).start()

    def send_l(src_slot, dst_slot, j, stream, device):
        copy(
            lbuf.at[src_slot, j], lbuf.at[dst_slot, j], ssem.at[stream, 1], lrecv.at[dst_slot, j],
            device,
        ).start()

    def wait_u(slot, i):
        copy(rows(slot, i), rows(slot, i), ssem.at[S_OWN, 0], urecv.at[slot, i], sibling).wait_recv()

    def wait_l(slot, j):
        copy(
            lbuf.at[slot, j], lbuf.at[slot, j], ssem.at[S_OWN, 1], lrecv.at[slot, j], sibling
        ).wait_recv()

    own_slot = INNER2 - (1 - ((k == 1) | (k == 2)).astype(jnp.int32))

    def send_own(send, i):
        send(OWN, own_slot, i, S_OWN, ahead)

        @pl.when(y < 3)
        def _():
            send(OWN, PREV, i, S_UP, up)

        @pl.when(y > 0)
        def _():
            send(OWN, NEXT, i, S_DOWN, down)

    def relay_first(send, wait, i):
        wait(OUTER, i)
        send(OUTER, OUTER2, i, S_OUTER, ahead)
        wait(INNER2, i)
        send(INNER2, INNER3, i, S_INNER2, right)

        @pl.when(edge)
        def _():
            send(INNER2, wrap_slot, i, S_WRAP_I, wrap_i)

    def relay_second(send, wait, i):
        wait(OUTER2, i)
        send(OUTER2, OUTER3, i, S_OUTER2, right)

        @pl.when(edge)
        def _():
            send(OUTER2, wrap_slot, i, S_WRAP_O, wrap_o)

    valid = (lax.broadcasted_iota(jnp.int32, (ROWS, 1), 0) < count_ref[0]).astype(F32)

    values = emb_ref[...].astype(F32)
    scaled = values * lax.rsqrt(jnp.mean(values * values, axis=-1, keepdims=True) + 1e-06)
    ubuf[OWN] = (scaled / math.sqrt(WIDTH)).astype(BF16)
    pl.semaphore_wait(barrier, 7 + jnp.where(edge, 1, 0) + jnp.where(edge & inner, 2, 0))
    copy(ubuf.at[OWN], sibu.at[0], ssem.at[S_SIB_OWN, 0], sibrecv.at[0], sibling).start()
    for i in range(2):
        send_own(send_u, i)
    for j in range(LN):
        lbuf[OWN, j] = (lab_ref[:, j * LANE : (j + 1) * LANE].astype(F32) * valid).astype(BF16)

    def wait_sib_u():
        copy(ubuf.at[OWN], sibu.at[0], ssem.at[S_SIB_OWN, 0], sibrecv.at[0], sibling).wait_recv()

    def affinity(tile, left_unit, slot):
        cosine = lax.dot_general(
            left_unit, ubuf[slot], (((1,), (1,)), ((), ())), preferred_element_type=F32
        )
        tiles[tile] = jnp.exp(sharpness * cosine).astype(BF16)

    def self_tile():
        cosine = lax.dot_general(
            ubuf[OWN], ubuf[OWN], (((1,), (1,)), ((), ())), preferred_element_type=F32
        )
        a = lax.broadcasted_iota(jnp.int32, (ROWS, ROWS), 0)
        b = lax.broadcasted_iota(jnp.int32, (ROWS, ROWS), 1)
        tiles[T_OWN] = jnp.where(a == b, 0.0, jnp.exp(sharpness * cosine)).astype(BF16)

    def product(tile, slot, j):
        return jnp.dot(tiles[tile], lbuf[slot, j], preferred_element_type=F32)

    def part(buf, j):
        return buf.at[j]

    def send_part(psend, precv, kind, j):
        copy(
            psend.at[j], precv.at[j], ssem.at[S_PART0 + kind, 0], prsem.at[kind, j], sibling
        ).start()

    def wait_part(precv, kind, j):
        copy(
            precv.at[j], precv.at[j], ssem.at[S_PART0 + kind, 0], prsem.at[kind, j], sibling
        ).wait_recv()

    def finish(w):
        total = jnp.zeros((ROWS, 1), F32)
        for j in range(LN):
            summed = acc[j]
            total = total + jnp.sum(summed * summed, axis=-1, keepdims=True)
        factor = keep_share * lax.rsqrt(total / CLASSES + 1e-06) * valid
        for j in range(LN):
            seed = lbuf[OWN, j].astype(F32)
            mixed = (acc[j] * factor + (1.0 - keep_share) * valid * seed).astype(BF16)

            @pl.when(w == 0)
            def _():
                lbuf[OWN, LN + j] = mixed

            @pl.when(w == 1)
            def _():
                out_ref[:, j * LANE : (j + 1) * LANE] = mixed

    def group_products(q):
        wait_l(NEXT, q)
        wait_l(PREV, q)

    @pl.when(inner)
    def _():
        def unit_step(i, _):
            relay_first(send_u, wait_u, i)
            copy(
                rows(OUTER, i), sibu.at[1, pl.ds(pl.multiple_of(i * UROWS, UROWS), UROWS)],
                ssem.at[S_SIB_OUTER, 0], sibrecv.at[1 + i], sibling,
            ).start()

            @pl.when(i < UN - 2)
            def _():
                send_own(send_u, i + 2)

            @pl.when(i >= UN - 2)
            def _():
                send_own(send_l, i - (UN - 2))

            @pl.when(i > 0)
            def _():
                relay_second(send_u, wait_u, i - 1)

            @pl.when(i == 2)
            def _():
                self_tile()
                wait_sib_u()
                affinity(T_SIB, sibu[0], OWN)

        lax.fori_loop(0, UN, unit_step, None)
        relay_second(send_u, wait_u, UN - 1)

        def tiles_0():
            for i in range(UN):
                copy(
                    rows(OUTER, i), sibu.at[1, pl.ds(i * UROWS, UROWS)], ssem.at[S_SIB_OUTER, 0],
                    sibrecv.at[1 + i], sibling,
                ).wait_recv()
            affinity(T_OUT, ubuf[OUTER], OWN)
            affinity(T_OUTSIB, sibu[1], OWN)
            affinity(T_OWN + 1, ubuf[OWN], OUTER)
            affinity(T_SIB + 1, sibu[0], OUTER)

        def tiles_1():
            affinity(T_OWN + 2, ubuf[OWN], INNER2)
            affinity(T_SIB + 2, sibu[0], INNER2)
            affinity(T_OUT + 1, ubuf[OUTER], INNER2)
            affinity(T_OWN + 3, ubuf[OWN], OUTER2)
            for slot in (INNER3, OUTER3):
                for i in range(UN):
                    wait_u(slot, i)

        def tiles_2():
            affinity(T_SIB + 3, sibu[0], sib_slot)
            affinity(T_OUT + 2, ubuf[OUTER], INNER3)
            affinity(T_OWN + 4, ubuf[OWN], OUTER3)
            affinity(T_OUT + 3, ubuf[OUTER], OUTER3)
            affinity(T_OUTSIB + 1, sibu[1], OUTER3)
            affinity(T_OUTSIB + 2, sibu[1], outsib_slot)
            for slot in (NEXT, PREV):
                for i in range(UN):
                    wait_u(slot, i)
            affinity(T_OWN + 5, ubuf[OWN], NEXT)
            affinity(T_OWN + 6, ubuf[OWN], PREV)

        def sweep(w, _):
            base = w * LN

            def combine(q):
                wait_part(precv1, 1, base + q)
                ssend[base + q] = (acco[q] + precv1[base + q]).astype(BF16)
                copy(
                    ssend.at[base + q], srecv.at[base + q], ssem.at[S_SUM, 0], srsem.at[base + q],
                    behind,
                ).start()
                wait_part(precv0, 0, base + q)
                acc[q] += precv0[base + q]

            def grouped(q):
                wait_l(NEXT, base + q)
                wait_l(PREV, base + q)
                acc[q] += product(T_OWN + 5, NEXT, base + q) + product(T_OWN + 6, PREV, base + q)

            def compute(q, _):
                j = base + q
                wait_l(INNER3, j)
                wait_l(OUTER3, j)
                psend1[j] = (
                    product(T_OUTSIB, OWN, j)
                    + product(T_OUTSIB + 1, OUTER3, j)
                    + product(T_OUTSIB + 2, outsib_slot, j)
                )
                send_part(psend1, precv1, 1, j)
                psend0[j] = (
                    product(T_SIB, OWN, j)
                    + product(T_SIB + 1, OUTER, j)
                    + product(T_SIB + 2, INNER2, j)
                    + product(T_SIB + 3, sib_slot, j)
                )
                send_part(psend0, precv0, 0, j)
                acco[q] = (
                    product(T_OUT, OWN, j)
                    + product(T_OUT + 1, INNER2, j)
                    + product(T_OUT + 2, INNER3, j)
                    + product(T_OUT + 3, OUTER3, j)
                )
                acc[q] = (
                    product(T_OWN, OWN, j)
                    + product(T_OWN + 1, OUTER, j)
                    + product(T_OWN + 2, INNER2, j)
                    + product(T_OWN + 3, OUTER2, j)
                    + product(T_OWN + 4, OUTER3, j)
                )

                @pl.when(q > 0)
                def _():
                    combine(q - 1)
                    grouped(q - 1)

            def step(t, _):
                @pl.when(t < LN)
                def _():
                    relay_first(send_l, wait_l, base + t)

                @pl.when(t < LN - 2)
                def _():
                    send_own(send_l, base + t + 2)

                @pl.when((t > 0) & (t <= LN))
                def _():
                    relay_second(send_l, wait_l, base + t - 1)

                first = w == 0
                pl.when(first & (t == 0))(tiles_0)
                pl.when(first & (t == 1))(tiles_1)
                pl.when(first & (t == 2))(tiles_2)
                low = t - 2 - jnp.where(first & (t >= 3) & (t <= 4), 1, 0)
                low = jnp.maximum(low, 0)
                high = t - 1 - jnp.where(first & (t >= 2) & (t <= 3), 1, 0)
                lax.fori_loop(low, jnp.maximum(high, low), compute, None)

            lax.fori_loop(0, LN + 2, step, None)
            combine(LN - 1)
            grouped(LN - 1)
            finish(w)

            @pl.when(w == 0)
            def _():
                for j in range(2):
                    send_own(send_l, LN + j)

        lax.fori_loop(0, 2, sweep, None)

    @pl.when(jnp.logical_not(inner))
    def _():
        def unit_step(i, _):
            send_own(send_u, i)

        lax.fori_loop(2, UN, unit_step, None)

        def label_step(j, _):
            send_own(send_l, j)

        lax.fori_loop(0, LN, label_step, None)
        self_tile()
        wait_sib_u()
        affinity(T_SIB, sibu[0], OWN)
        for slot in (NEXT, PREV):
            for i in range(UN):
                wait_u(slot, i)
        affinity(T_OWN + 5, ubuf[OWN], NEXT)
        affinity(T_OWN + 6, ubuf[OWN], PREV)

        def sweep(w, _):
            base = w * LN

            def near(q, _):
                j = base + q
                psend0[j] = product(T_SIB, OWN, j)
                send_part(psend0, precv0, 0, j)
                acc[q] = product(T_OWN, OWN, j)

            lax.fori_loop(0, LN, near, None)

            def far(q, _):
                j = base + q
                wait_part(precv0, 0, j)
                wait_l(NEXT, j)
                wait_l(PREV, j)
                grouped = product(T_OWN + 5, NEXT, j) + product(T_OWN + 6, PREV, j)
                copy(
                    srecv.at[j], srecv.at[j], ssem.at[S_SUM, 0], srsem.at[j], ahead
                ).wait_recv()
                acc[q] += precv0[j] + grouped + srecv[j].astype(F32)

            lax.fori_loop(0, LN, far, None)
            finish(w)

            @pl.when(w == 0)
            def _():
                lax.fori_loop(LN, 2 * LN, label_step, None)

        lax.fori_loop(0, 2, sweep, None)

    def sent(slot, stream):
        copy(
            ubuf.at[slot], ubuf.at[slot], ssem.at[stream, 0], urecv.at[slot, 0], sibling
        ).wait_send()
        copy(
            lbuf.at[slot], lbuf.at[slot], ssem.at[stream, 1], lrecv.at[slot, 0], sibling
        ).wait_send()

    sent(OWN, S_OWN)
    pl.when(y < 3)(lambda: sent(OWN, S_UP))
    pl.when(y > 0)(lambda: sent(OWN, S_DOWN))
    copy(ubuf.at[OWN], sibu.at[0], ssem.at[S_SIB_OWN, 0], sibrecv.at[0], sibling).wait_send()
    copy(psend0, precv0, ssem.at[S_PART0, 0], prsem.at[0, 0], sibling).wait_send()

    @pl.when(inner)
    def _():
        sent(OUTER, S_OUTER)
        sent(INNER2, S_INNER2)
        sent(OUTER2, S_OUTER2)
        copy(ubuf.at[OUTER], sibu.at[1], ssem.at[S_SIB_OUTER, 0], sibrecv.at[1], sibling).wait_send()
        copy(psend1, precv1, ssem.at[S_PART1, 0], prsem.at[1, 0], sibling).wait_send()
        copy(ssend, srecv, ssem.at[S_SUM, 0], srsem.at[0], behind).wait_send()

    @pl.when(edge & inner)
    def _():
        sent(INNER2, S_WRAP_I)
        sent(OUTER2, S_WRAP_O)


def body(embeddings, labels, cluster_rows):
    vmem = pl.BlockSpec(memory_space=pltpu.VMEM)
    part = pltpu.VMEM((2 * LN, ROWS, LANE), F32)
    half = pltpu.VMEM((2 * LN, ROWS, LANE), BF16)
    return pl.pallas_call(
        kernel,
        out_shape=jax.ShapeDtypeStruct((ROWS, CLASSES), BF16),
        in_specs=[pl.BlockSpec(memory_space=pltpu.SMEM), vmem, vmem],
        out_specs=vmem,
        scratch_shapes=[
            pltpu.VMEM((SLOTS, ROWS, WIDTH), BF16),
            pltpu.VMEM((SLOTS, 2 * LN, ROWS, LANE), BF16),
            pltpu.VMEM((2, ROWS, WIDTH), BF16),
            pltpu.VMEM((N_TILES, ROWS, ROWS), BF16),
            pltpu.VMEM((LN, ROWS, LANE), F32),
            pltpu.VMEM((LN, ROWS, LANE), F32),
            part, part, part, part, half, half,
            pltpu.SemaphoreType.DMA((13, 2)),
            pltpu.SemaphoreType.DMA((SLOTS, UN)),
            pltpu.SemaphoreType.DMA((SLOTS, 2 * LN)),
            pltpu.SemaphoreType.DMA((1 + UN,)),
            pltpu.SemaphoreType.DMA((2, 2 * LN)),
            pltpu.SemaphoreType.DMA((2 * LN,)),
        ],
        compiler_params=pltpu.CompilerParams(
            collective_id=0, has_side_effects=True, vmem_limit_bytes=60 * 2**20
        ),
        cost_estimate=pl.CostEstimate(
            flops=14 * 10**9, bytes_accessed=2 * 10**6, transcendentals=3 * 10**6
        ),
    )(cluster_rows, embeddings, labels)


def solution(mesh):
    placed = (P(("grp", "dev"), None), P(("grp", "dev"), None), P(("grp", "dev")))
    return jax.shard_map(
        body, mesh=mesh, in_specs=placed, out_specs=P(("grp", "dev"), None), check_vma=False
    )
```

```python
import functools
import math

import jax
import jax.numpy as jnp
from jax import lax
from jax.experimental import pallas as pl
from jax.experimental.pallas import tpu as pltpu
from jax.sharding import PartitionSpec as P

MESH = pl.DeviceIdType.MESH
F32 = jnp.float32
BF16 = jnp.bfloat16

sharpness = 25.0
keep_share = 0.8

ROWS = 384
WIDTH = 768
CLASSES = 896
LANE = 128
UN = 6
UROWS = ROWS // UN
LN = CLASSES // LANE

OWN, OUTER, INNER2, OUTER2, INNER3, OUTER3, NEXT, PREV = range(8)
SLOTS = 8

(S_OWN, S_UP, S_DOWN, S_OUTER, S_INNER2, S_OUTER2, S_WRAP_I, S_WRAP_O, S_SIB_OWN, S_SIB_OUTER, S_PART0, S_PART1,
 S_SUM, S_ASIDE, S_ONWARD) = range(15)
NORM_STEP = 10
DETOUR = 6

T_OWN, T_SIB, T_OUT, T_OUTSIB = 0, 7, 11, 15
N_TILES = 18
OWN_SOURCES = (OWN, OUTER, INNER2, OUTER2, OUTER3, NEXT, PREV)
SIB_SOURCES = (OWN, OUTER, INNER2, None)
OUT_SOURCES = (OWN, INNER2, INNER3, OUTER3)
OUTSIB_SOURCES = (OWN, OUTER3, None)


def kernel(
    count_ref, emb_ref, lab_ref, out_ref,
    ubuf, lbuf, sibu, tiles, acc, acco, psend0, psend1, precv0, precv1, ssend, srecv, aside, norm,
    ssem, urecv, lrecv, sibrecv, prsem, srsem, asidesem, normrecv,
):
    g, d = lax.axis_index("grp"), lax.axis_index("dev")
    x, k, c = d // 8, (d // 2) % 4, d % 2
    z, y = (g // 4) * 4 + k, g % 4
    s = 1 - 2 * (k // 2)
    inner = (k == 1) | (k == 2)
    edge = (y == 0) | (y == 3)

    def at(x, y, z, c):
        x, y, z = (x + 4) % 4, (y + 4) % 4, (z + 16) % 8
        return ((z // 4) * 4 + y, x * 8 + (z % 4) * 2 + c)

    sibling = at(x, y, z, 1 - c)
    ahead = at(x, y, z + s, c)
    behind = at(x, y, z - s, c)
    up, down = at(x, y + 1, z, c), at(x, y - 1, z, c)
    right, left = at(x + s, y, z, c), at(x - s, y, z, c)
    wrap_i = at(x, 3 - y, z + s + 4, c)
    wrap_o = at(x, 3 - y, z + 2 * s + 4, c)
    wrap_slot = NEXT + y // 3
    relay = at(x, 3 - y, z + 4 + s * (2 - ((k == 1) | (k == 2)).astype(jnp.int32)), c)
    side = (c + k // 2) % 2
    sib_slot = OUTER2 + 2 * side
    outsib_slot = INNER2 + 2 * side

    beside = at(x, 1 + y // 3, z, c)
    served = at(x, 3 - 3 * (y // 2), z + s + 4, c)
    served_slot = NEXT + y // 2
    server = at(x, 1 + (3 - y) // 3, z + s + 4, c)

    barrier = pltpu.get_barrier_semaphore()

    def greet(device):
        pl.semaphore_signal(barrier, inc=1, device_id=device, device_id_type=MESH)

    for device in (sibling, ahead, behind, up, down, right, left):
        greet(device)

    @pl.when(edge)
    def _():
        greet(relay)

    @pl.when(edge & inner)
    def _():
        greet(wrap_i)
        greet(wrap_o)
        greet(server)

    @pl.when(jnp.logical_not(edge) & inner)
    def _():
        greet(served)

    def copy(src, dst, send_sem, recv_sem, device):
        return pltpu.make_async_remote_copy(
            src_ref=src, dst_ref=dst, send_sem=send_sem, recv_sem=recv_sem, device_id=device,
            device_id_type=MESH,
        )

    def rows(slot, i):
        return ubuf.at[slot, pl.ds(pl.multiple_of(i * UROWS, UROWS), UROWS)]

    def send_u(src_slot, dst_slot, i, stream, device):
        copy(
            rows(src_slot, i), rows(dst_slot, i), ssem.at[stream, 0], urecv.at[dst_slot, i], device
        ).start()

    def send_l(src_slot, dst_slot, j, stream, device):
        copy(
            lbuf.at[src_slot, j], lbuf.at[dst_slot, j], ssem.at[stream, 1], lrecv.at[dst_slot, j],
            device,
        ).start()

    def wait_u(slot, i):
        copy(rows(slot, i), rows(slot, i), ssem.at[S_OWN, 0], urecv.at[slot, i], sibling).wait_recv()

    def wait_l(slot, j):
        copy(
            lbuf.at[slot, j], lbuf.at[slot, j], ssem.at[S_OWN, 1], lrecv.at[slot, j], sibling
        ).wait_recv()

    def send_norm(src_slot, dst_slot, _, stream, device):
        copy(
            norm.at[src_slot], norm.at[dst_slot], ssem.at[stream, 2], normrecv.at[dst_slot], device
        ).start()

    def wait_norm(slot, _):
        copy(
            norm.at[slot], norm.at[slot], ssem.at[S_OWN, 2], normrecv.at[slot], sibling
        ).wait_recv()

    own_slot = INNER2 - (1 - ((k == 1) | (k == 2)).astype(jnp.int32))

    def send_own(send, i):
        send(OWN, own_slot, i, S_OWN, ahead)

        @pl.when(y < 3)
        def _():
            send(OWN, PREV, i, S_UP, up)

        @pl.when(y > 0)
        def _():
            send(OWN, NEXT, i, S_DOWN, down)

    def relay_outer(send, wait, i):
        wait(OUTER, i)
        send(OUTER, OUTER2, i, S_OUTER, ahead)

    def relay_inner(send, wait, i):
        wait(INNER2, i)
        send(INNER2, INNER3, i, S_INNER2, right)

    def wrap_inner(send, i):
        @pl.when(edge)
        def _():
            send(INNER2, wrap_slot, i, S_WRAP_I, wrap_i)

    def relay_second(send, wait, i):
        wait(OUTER2, i)
        send(OUTER2, OUTER3, i, S_OUTER2, right)

        @pl.when(edge)
        def _():
            send(OUTER2, wrap_slot, i, S_WRAP_O, wrap_o)

    acc[...] = jnp.zeros_like(acc)
    valid = (lax.broadcasted_iota(jnp.int32, (ROWS, 1), 0) < count_ref[0]).astype(F32)

    values = emb_ref[...].astype(F32)
    scaled = values * lax.rsqrt(jnp.mean(values * values, axis=-1, keepdims=True) + 1e-06)
    ubuf[OWN] = (scaled / math.sqrt(WIDTH)).astype(BF16)
    pl.semaphore_wait(
        barrier, 7 + jnp.where(inner, jnp.where(edge, 4, 1), jnp.where(edge, 1, 0))
    )
    copy(ubuf.at[OWN], sibu.at[0], ssem.at[S_SIB_OWN, 0], sibrecv.at[0], sibling).start()
    for i in range(2):
        send_own(send_u, i)
    for j in range(LN):
        lbuf[OWN, j] = (lab_ref[:, j * LANE : (j + 1) * LANE].astype(F32) * valid).astype(BF16)

    def wait_sib_u():
        copy(ubuf.at[OWN], sibu.at[0], ssem.at[S_SIB_OWN, 0], sibrecv.at[0], sibling).wait_recv()

    def affinity(tile, left_unit, slot):
        cosine = lax.dot_general(
            left_unit, ubuf[slot], (((1,), (1,)), ((), ())), preferred_element_type=F32
        )
        tiles[tile] = jnp.exp(sharpness * cosine).astype(BF16)

    def self_tile():
        cosine = lax.dot_general(
            ubuf[OWN], ubuf[OWN], (((1,), (1,)), ((), ())), preferred_element_type=F32
        )
        tiles[T_OWN] = jnp.where(diagonal(), 0.0, jnp.exp(sharpness * cosine)).astype(BF16)

    def product(tile, slot, j):
        return jnp.dot(tiles[tile], lbuf[slot, j], preferred_element_type=F32)

    def send_part(psend, precv, kind, j):
        copy(
            psend.at[j], precv.at[j], ssem.at[S_PART0 + kind, 0], prsem.at[kind, j], sibling
        ).start()

    def wait_part(precv, kind, j):
        copy(
            precv.at[j], precv.at[j], ssem.at[S_PART0 + kind, 0], prsem.at[kind, j], sibling
        ).wait_recv()

    def row_factor():
        total = jnp.zeros((ROWS, 1), F32)
        for j in range(LN):
            summed = acc[j]
            total = total + jnp.sum(summed * summed, axis=-1, keepdims=True)
        return keep_share * lax.rsqrt(total / CLASSES + 1e-06) * valid

    def diagonal():
        a = lax.broadcasted_iota(jnp.int32, (ROWS, ROWS), 0)
        return a == lax.broadcasted_iota(jnp.int32, (ROWS, ROWS), 1)

    def share_factor():
        row = jnp.sum(jnp.where(diagonal(), row_factor(), 0.0), axis=0, keepdims=True)
        norm[OWN] = jnp.broadcast_to(row, (8, ROWS))
        send_own(send_norm, 0)

    def finish():
        factor = row_factor()
        for j in range(LN):
            seed = lbuf[OWN, j].astype(F32)
            mixed = acc[j] * factor + (1.0 - keep_share) * seed
            out_ref[:, j * LANE : (j + 1) * LANE] = mixed.astype(BF16)

    def send_sum(q):
        lbuf[OWN, LN + q] = acc[q].astype(BF16)
        send_own(send_l, LN + q)

    def scale(tile, slot):
        tiles[tile] = (tiles[tile].astype(F32) * norm[slot, 0:1]).astype(BF16)

    @pl.when(inner)
    def _():
        def unit_step(i, _):
            relay_outer(send_u, wait_u, i)
            relay_inner(send_u, wait_u, i)
            wrap_inner(send_u, i)
            copy(
                rows(OUTER, i), sibu.at[1, pl.ds(pl.multiple_of(i * UROWS, UROWS), UROWS)],
                ssem.at[S_SIB_OUTER, 0], sibrecv.at[1 + i], sibling,
            ).start()

            @pl.when(i < UN - 2)
            def _():
                send_own(send_u, i + 2)

            @pl.when(i >= UN - 2)
            def _():
                send_own(send_l, i - (UN - 2))

            @pl.when(i > 0)
            def _():
                relay_second(send_u, wait_u, i - 1)

            @pl.when(i == 2)
            def _():
                self_tile()
                wait_sib_u()
                affinity(T_SIB, sibu[0], OWN)

        lax.fori_loop(0, UN, unit_step, None)
        relay_second(send_u, wait_u, UN - 1)

        def tiles_0():
            for i in range(UN):
                copy(
                    rows(OUTER, i), sibu.at[1, pl.ds(i * UROWS, UROWS)], ssem.at[S_SIB_OUTER, 0],
                    sibrecv.at[1 + i], sibling,
                ).wait_recv()
            affinity(T_OUT, ubuf[OUTER], OWN)
            affinity(T_OUTSIB, sibu[1], OWN)
            affinity(T_OWN + 1, ubuf[OWN], OUTER)
            affinity(T_SIB + 1, sibu[0], OUTER)

        def tiles_1():
            affinity(T_OWN + 2, ubuf[OWN], INNER2)
            affinity(T_SIB + 2, sibu[0], INNER2)
            affinity(T_OUT + 1, ubuf[OUTER], INNER2)
            affinity(T_OWN + 3, ubuf[OWN], OUTER2)
            for slot in (INNER3, OUTER3):
                for i in range(UN):
                    wait_u(slot, i)

        def tiles_2():
            affinity(T_SIB + 3, sibu[0], sib_slot)
            affinity(T_OUT + 2, ubuf[OUTER], INNER3)
            affinity(T_OWN + 4, ubuf[OWN], OUTER3)
            affinity(T_OUT + 3, ubuf[OUTER], OUTER3)
            affinity(T_OUTSIB + 1, sibu[1], OUTER3)
            affinity(T_OUTSIB + 2, sibu[1], outsib_slot)
            for slot in (NEXT, PREV):
                for i in range(UN):
                    wait_u(slot, i)
            affinity(T_OWN + 5, ubuf[OWN], NEXT)
            affinity(T_OWN + 6, ubuf[OWN], PREV)

        def scale_near():
            for i, slot in ((0, OWN), (1, OUTER), (2, INNER2)):
                scale(T_OWN + i, slot)
                scale(T_SIB + i, slot)
            scale(T_OUT, OWN)
            scale(T_OUT + 1, INNER2)
            scale(T_OUTSIB, OWN)

        def scale_far():
            scale(T_OWN + 3, OUTER2)
            scale(T_OWN + 4, OUTER3)
            scale(T_SIB + 3, sib_slot)
            scale(T_OUT + 2, INNER3)
            scale(T_OUT + 3, OUTER3)
            scale(T_OUTSIB + 1, OUTER3)
            scale(T_OUTSIB + 2, outsib_slot)
            scale(T_OWN + 5, NEXT)
            scale(T_OWN + 6, PREV)

        def combine(q, j):
            wait_part(precv1, 1, j)
            ssend[j] = (acco[q] + precv1[j]).astype(BF16)

            copy(ssend.at[j], srecv.at[j], ssem.at[S_SUM, 0], srsem.at[j], behind).start()
            wait_part(precv0, 0, j)
            acc[q] += precv0[j]

        def onward(j):
            copy(
                aside.at[j], aside.at[j], ssem.at[S_ASIDE, 0], asidesem.at[j], sibling
            ).wait_recv()
            copy(
                aside.at[j], lbuf.at[served_slot, j], ssem.at[S_ONWARD, 0],
                lrecv.at[served_slot, j], served,
            ).start()

        def grouped(q, j):
            wait_l(NEXT, j)
            wait_l(PREV, j)
            acc[q] += product(T_OWN + 5, NEXT, j) + product(T_OWN + 6, PREV, j)

        def compute(j, _):
            second = j // LN
            q = j - second * LN
            kept = jnp.where(second == 0, 0.0, 1.0 - keep_share)
            wait_l(INNER3, j)
            wait_l(OUTER3, j)
            psend1[j] = (
                product(T_OUTSIB, OWN, j)
                + product(T_OUTSIB + 1, OUTER3, j)
                + product(T_OUTSIB + 2, outsib_slot, j)
            )
            send_part(psend1, precv1, 1, j)
            psend0[j] = (
                product(T_SIB, OWN, j)
                + product(T_SIB + 1, OUTER, j)
                + product(T_SIB + 2, INNER2, j)
                + product(T_SIB + 3, sib_slot, j)
            )
            send_part(psend0, precv0, 0, j)
            acco[q] = (
                product(T_OUT, OWN, j)
                + product(T_OUT + 1, INNER2, j)
                + product(T_OUT + 2, INNER3, j)
                + product(T_OUT + 3, OUTER3, j)
            )
            acc[q] = acc[q] * kept + (
                product(T_OWN, OWN, j)
                + product(T_OWN + 1, OUTER, j)
                + product(T_OWN + 2, INNER2, j)
                + product(T_OWN + 3, OUTER2, j)
                + product(T_OWN + 4, OUTER3, j)
            )
            combine(q, j)

            @pl.when(q > 1)
            def _():
                grouped(q - 2, j - 2)

        def done(n):
            one = jnp.where(n >= 4, n - 1, jnp.where(n == 3, 1, 0))
            return jnp.where(n < 9, one, jnp.clip(7 + 2 * (n - 11), 7, 14))

        def step(n, _):
            @pl.when(n < 2 * LN)
            def _():
                relay_outer(send_l, wait_l, n)

            @pl.when(n < LN - 2)
            def _():
                send_own(send_l, n + 2)

            @pl.when((n >= LN - 2) & (n < 2 * LN - 2))
            def _():
                send_sum(n - (LN - 2))

            @pl.when(n < 2 * LN)
            def _():
                relay_inner(send_l, wait_l, n)

                @pl.when(n - (n // LN) * LN >= DETOUR)
                def _():
                    wrap_inner(send_l, n)

                @pl.when(edge & (n - (n // LN) * LN < DETOUR))
                def _():
                    copy(
                        lbuf.at[INNER2, n], aside.at[n], ssem.at[S_ASIDE, 1], asidesem.at[n],
                        beside,
                    ).start()

            @pl.when((n > 0) & (n <= 2 * LN))
            def _():
                relay_second(send_l, wait_l, n - 1)

            late = n - 2

            @pl.when((n >= 2) & (late - (late // LN) * LN < DETOUR) & jnp.logical_not(edge))
            def _():
                onward(late)

            pl.when(n == 0)(tiles_0)
            pl.when(n == 1)(tiles_1)
            pl.when(n == 2)(tiles_2)

            @pl.when(n == NORM_STEP)
            def _():
                relay_outer(send_norm, wait_norm, 0)
                relay_inner(send_norm, wait_norm, 0)
                wrap_inner(send_norm, 0)

            @pl.when(n == NORM_STEP + 1)
            def _():
                relay_second(send_norm, wait_norm, 0)
                scale_near()

            @pl.when(n == NORM_STEP + 2)
            def _():
                for slot in (INNER3, OUTER3, NEXT, PREV):
                    wait_norm(slot, 0)
                scale_far()

            lax.fori_loop(jnp.where(n == 0, 0, done(n - 1)), done(n), compute, None)

            @pl.when(n == LN + 1)
            def _():
                grouped(LN - 2, LN - 2)
                grouped(LN - 1, LN - 1)
                share_factor()

        lax.fori_loop(0, 2 * LN + 2, step, None)
        grouped(LN - 2, 2 * LN - 2)
        grouped(LN - 1, 2 * LN - 1)

    @pl.when(jnp.logical_not(inner))
    def _():
        def unit_step(i, _):
            send_own(send_u, i)

        lax.fori_loop(2, UN, unit_step, None)

        def label_step(j, _):
            send_own(send_l, j)

        lax.fori_loop(0, LN, label_step, None)
        self_tile()
        wait_sib_u()
        affinity(T_SIB, sibu[0], OWN)
        for slot in (NEXT, PREV):
            for i in range(UN):
                wait_u(slot, i)
        affinity(T_OWN + 5, ubuf[OWN], NEXT)
        affinity(T_OWN + 6, ubuf[OWN], PREV)

        def near(j, _):
            second = j // LN
            q = j - second * LN
            psend0[j] = product(T_SIB, OWN, j)
            send_part(psend0, precv0, 0, j)
            kept = jnp.where(second == 0, 0.0, 1.0 - keep_share)
            acc[q] = acc[q] * kept + product(T_OWN, OWN, j)

        def far(j, _):
            q = j - (j // LN) * LN
            wait_part(precv0, 0, j)
            wait_l(NEXT, j)
            wait_l(PREV, j)
            grouped = product(T_OWN + 5, NEXT, j) + product(T_OWN + 6, PREV, j)
            copy(srecv.at[j], srecv.at[j], ssem.at[S_SUM, 0], srsem.at[j], ahead).wait_recv()
            acc[q] += precv0[j] + grouped + srecv[j].astype(F32)
            pl.when(j < LN)(lambda: send_sum(q))

        lax.fori_loop(0, LN, near, None)
        lax.fori_loop(0, LN, far, None)
        share_factor()
        scale(T_OWN, OWN)
        scale(T_SIB, OWN)
        lax.fori_loop(LN, 2 * LN, near, None)
        wait_norm(NEXT, 0)
        wait_norm(PREV, 0)
        scale(T_OWN + 5, NEXT)
        scale(T_OWN + 6, PREV)
        lax.fori_loop(LN, 2 * LN, far, None)

    finish()

    def sent(slot, stream):
        copy(
            ubuf.at[slot], ubuf.at[slot], ssem.at[stream, 0], urecv.at[slot, 0], sibling
        ).wait_send()
        copy(
            lbuf.at[slot], lbuf.at[slot], ssem.at[stream, 1], lrecv.at[slot, 0], sibling
        ).wait_send()
        copy(norm.at[slot], norm.at[slot], ssem.at[stream, 2], normrecv.at[slot], sibling).wait_send()

    sent(OWN, S_OWN)
    pl.when(y < 3)(lambda: sent(OWN, S_UP))
    pl.when(y > 0)(lambda: sent(OWN, S_DOWN))
    copy(ubuf.at[OWN], sibu.at[0], ssem.at[S_SIB_OWN, 0], sibrecv.at[0], sibling).wait_send()
    copy(psend0, precv0, ssem.at[S_PART0, 0], prsem.at[0, 0], sibling).wait_send()

    @pl.when(inner)
    def _():
        sent(OUTER, S_OUTER)
        sent(INNER2, S_INNER2)
        sent(OUTER2, S_OUTER2)
        copy(ubuf.at[OUTER], sibu.at[1], ssem.at[S_SIB_OUTER, 0], sibrecv.at[1], sibling).wait_send()
        copy(psend1, precv1, ssem.at[S_PART1, 0], prsem.at[1, 0], sibling).wait_send()

    @pl.when(inner)
    def _():
        copy(ssend, srecv, ssem.at[S_SUM, 0], srsem.at[0], behind).wait_send()

    @pl.when(inner & jnp.logical_not(edge))
    def _():
        some = aside.at[pl.ds(0, 2 * DETOUR)]
        copy(some, some, ssem.at[S_ONWARD, 0], asidesem.at[0], sibling).wait_send()

    @pl.when(edge & inner)
    def _():
        sent(OUTER2, S_WRAP_O)
        block = ubuf.at[INNER2]
        copy(block, block, ssem.at[S_WRAP_I, 0], urecv.at[INNER2, 0], sibling).wait_send()
        some = lbuf.at[INNER2, pl.ds(0, 2 * (LN - DETOUR))]
        copy(some, some, ssem.at[S_WRAP_I, 1], lrecv.at[INNER2, 0], sibling).wait_send()
        row = norm.at[INNER2]
        copy(row, row, ssem.at[S_WRAP_I, 2], normrecv.at[INNER2], sibling).wait_send()
        some = lbuf.at[INNER2, pl.ds(0, 2 * DETOUR)]
        copy(some, some, ssem.at[S_ASIDE, 1], lrecv.at[INNER2, 0], sibling).wait_send()


def body(embeddings, labels, cluster_rows):
    vmem = pl.BlockSpec(memory_space=pltpu.VMEM)
    part = pltpu.VMEM((2 * LN, ROWS, LANE), F32)
    half = pltpu.VMEM((2 * LN, ROWS, LANE), BF16)
    return pl.pallas_call(
        kernel,
        out_shape=jax.ShapeDtypeStruct((ROWS, CLASSES), BF16),
        in_specs=[pl.BlockSpec(memory_space=pltpu.SMEM), vmem, vmem],
        out_specs=vmem,
        scratch_shapes=[
            pltpu.VMEM((SLOTS, ROWS, WIDTH), BF16),
            pltpu.VMEM((SLOTS, 2 * LN, ROWS, LANE), BF16),
            pltpu.VMEM((2, ROWS, WIDTH), BF16),
            pltpu.VMEM((N_TILES, ROWS, ROWS), BF16),
            pltpu.VMEM((LN, ROWS, LANE), F32),
            pltpu.VMEM((LN, ROWS, LANE), F32),
            part, part, part, part, half, half, half,
            pltpu.VMEM((SLOTS, 8, ROWS), F32),
            pltpu.SemaphoreType.DMA((15, 3)),
            pltpu.SemaphoreType.DMA((SLOTS, UN)),
            pltpu.SemaphoreType.DMA((SLOTS, 2 * LN)),
            pltpu.SemaphoreType.DMA((1 + UN,)),
            pltpu.SemaphoreType.DMA((2, 2 * LN)),
            pltpu.SemaphoreType.DMA((2 * LN,)),
            pltpu.SemaphoreType.DMA((2 * LN,)),
            pltpu.SemaphoreType.DMA((SLOTS,)),
        ],
        compiler_params=pltpu.CompilerParams(
            collective_id=0, has_side_effects=True, vmem_limit_bytes=60 * 2**20
        ),
        cost_estimate=pl.CostEstimate(
            flops=14 * 10**9, bytes_accessed=2 * 10**6, transcendentals=3 * 10**6
        ),
    )(cluster_rows, embeddings, labels)


def solution(mesh):
    placed = (P(("grp", "dev"), None), P(("grp", "dev"), None), P(("grp", "dev")))
    return jax.shard_map(
        body, mesh=mesh, in_specs=placed, out_specs=P(("grp", "dev"), None), check_vma=False
    )
```

```python
import functools
import math

import jax
import jax.numpy as jnp
from jax import lax
from jax.experimental import pallas as pl
from jax.experimental.pallas import tpu as pltpu
from jax.sharding import PartitionSpec as P

MESH = pl.DeviceIdType.MESH
F32 = jnp.float32
BF16 = jnp.bfloat16

sharpness = 25.0
keep_share = 0.8

ROWS = 384
WIDTH = 768
CLASSES = 896
LANE = 128
UN = 6
UROWS = ROWS // UN
LN = CLASSES // LANE

OWN, OUTER, INNER2, OUTER2, INNER3, OUTER3, NEXT, PREV = range(8)
SLOTS = 8

(S_OWN, S_UP, S_DOWN, S_OUTER, S_INNER2, S_OUTER2, S_WRAP_I, S_WRAP_O, S_SIB_OWN, S_SIB_OUTER, S_PART0, S_PART1,
 S_SUM, S_ASIDE, S_ONWARD) = range(15)
NORM_STEP = 9
DETOUR = 13

T_OWN, T_SIB, T_OUT, T_OUTSIB = 0, 7, 11, 15
N_TILES = 18
OWN_SOURCES = (OWN, OUTER, INNER2, OUTER2, OUTER3, NEXT, PREV)
SIB_SOURCES = (OWN, OUTER, INNER2, None)
OUT_SOURCES = (OWN, INNER2, INNER3, OUTER3)
OUTSIB_SOURCES = (OWN, OUTER3, None)


def kernel(
    count_ref, emb_ref, lab_ref, out_ref,
    ubuf, lbuf, sibu, tiles, acc, acco, psend0, psend1, precv0, precv1, ssend, srecv, aside, asideu, norm,
    ssem, urecv, lrecv, sibrecv, prsem, srsem, asidesem, asideusem, normrecv,
):
    g, d = lax.axis_index("grp"), lax.axis_index("dev")
    x, k, c = d // 8, (d // 2) % 4, d % 2
    z, y = (g // 4) * 4 + k, g % 4
    s = 1 - 2 * (k // 2)
    inner = (k == 1) | (k == 2)
    edge = (y == 0) | (y == 3)

    def at(x, y, z, c):
        x, y, z = (x + 4) % 4, (y + 4) % 4, (z + 16) % 8
        return ((z // 4) * 4 + y, x * 8 + (z % 4) * 2 + c)

    sibling = at(x, y, z, 1 - c)
    ahead = at(x, y, z + s, c)
    behind = at(x, y, z - s, c)
    up, down = at(x, y + 1, z, c), at(x, y - 1, z, c)
    right, left = at(x + s, y, z, c), at(x - s, y, z, c)
    wrap_i = at(x, 3 - y, z + s + 4, c)
    wrap_o = at(x, 3 - y, z + 2 * s + 4, c)
    wrap_slot = NEXT + y // 3
    relay = at(x, 3 - y, z + 4 + s * (2 - ((k == 1) | (k == 2)).astype(jnp.int32)), c)
    side = (c + k // 2) % 2
    sib_slot = OUTER2 + 2 * side
    outsib_slot = INNER2 + 2 * side

    beside = at(x, 1 + y // 3, z, c)
    served = at(x, 3 - 3 * (y // 2), z + s + 4, c)
    served_slot = NEXT + y // 2
    server = at(x, 1 + (3 - y) // 3, z + s + 4, c)

    barrier = pltpu.get_barrier_semaphore()

    def greet(device):
        pl.semaphore_signal(barrier, inc=1, device_id=device, device_id_type=MESH)

    for device in (sibling, ahead, behind, up, down, right, left):
        greet(device)

    @pl.when(edge)
    def _():
        greet(relay)

    @pl.when(edge & inner)
    def _():
        greet(wrap_i)
        greet(wrap_o)
        greet(server)

    @pl.when(jnp.logical_not(edge) & inner)
    def _():
        greet(served)

    def copy(src, dst, send_sem, recv_sem, device):
        return pltpu.make_async_remote_copy(
            src_ref=src, dst_ref=dst, send_sem=send_sem, recv_sem=recv_sem, device_id=device,
            device_id_type=MESH,
        )

    def rows(slot, i):
        return ubuf.at[slot, pl.ds(pl.multiple_of(i * UROWS, UROWS), UROWS)]

    def send_u(src_slot, dst_slot, i, stream, device):
        copy(
            rows(src_slot, i), rows(dst_slot, i), ssem.at[stream, 0], urecv.at[dst_slot, i], device
        ).start()

    def send_l(src_slot, dst_slot, j, stream, device):
        copy(
            lbuf.at[src_slot, j], lbuf.at[dst_slot, j], ssem.at[stream, 1], lrecv.at[dst_slot, j],
            device,
        ).start()

    def wait_u(slot, i):
        copy(rows(slot, i), rows(slot, i), ssem.at[S_OWN, 0], urecv.at[slot, i], sibling).wait_recv()

    def wait_l(slot, j):
        copy(
            lbuf.at[slot, j], lbuf.at[slot, j], ssem.at[S_OWN, 1], lrecv.at[slot, j], sibling
        ).wait_recv()

    def send_norm(src_slot, dst_slot, _, stream, device):
        copy(
            norm.at[src_slot], norm.at[dst_slot], ssem.at[stream, 2], normrecv.at[dst_slot], device
        ).start()

    def wait_norm(slot, _):
        copy(
            norm.at[slot], norm.at[slot], ssem.at[S_OWN, 2], normrecv.at[slot], sibling
        ).wait_recv()

    own_slot = INNER2 - (1 - ((k == 1) | (k == 2)).astype(jnp.int32))

    def send_own(send, i):
        send(OWN, own_slot, i, S_OWN, ahead)

        @pl.when(y < 3)
        def _():
            send(OWN, PREV, i, S_UP, up)

        @pl.when(y > 0)
        def _():
            send(OWN, NEXT, i, S_DOWN, down)

    def relay_outer(send, wait, i):
        wait(OUTER, i)
        send(OUTER, OUTER2, i, S_OUTER, ahead)

    def relay_inner(send, wait, i):
        wait(INNER2, i)
        send(INNER2, INNER3, i, S_INNER2, right)

    def wrap_inner(send, i):
        @pl.when(edge)
        def _():
            send(INNER2, wrap_slot, i, S_WRAP_I, wrap_i)

    def relay_second(send, wait, i):
        wait(OUTER2, i)
        send(OUTER2, OUTER3, i, S_OUTER2, right)

        @pl.when(edge)
        def _():
            send(OUTER2, wrap_slot, i, S_WRAP_O, wrap_o)

    acc[...] = jnp.zeros_like(acc)
    valid = (lax.broadcasted_iota(jnp.int32, (ROWS, 1), 0) < count_ref[0]).astype(F32)

    values = emb_ref[...].astype(F32)
    scaled = values * lax.rsqrt(jnp.mean(values * values, axis=-1, keepdims=True) + 1e-06)
    ubuf[OWN] = (scaled / math.sqrt(WIDTH)).astype(BF16)
    pl.semaphore_wait(
        barrier, 7 + jnp.where(inner, jnp.where(edge, 4, 1), jnp.where(edge, 1, 0))
    )
    copy(ubuf.at[OWN], sibu.at[0], ssem.at[S_SIB_OWN, 0], sibrecv.at[0], sibling).start()
    for i in range(2):
        send_own(send_u, i)
    for j in range(LN):
        lbuf[OWN, j] = (lab_ref[:, j * LANE : (j + 1) * LANE].astype(F32) * valid).astype(BF16)

    def wait_sib_u():
        copy(ubuf.at[OWN], sibu.at[0], ssem.at[S_SIB_OWN, 0], sibrecv.at[0], sibling).wait_recv()

    def affinity(tile, left_unit, slot):
        cosine = lax.dot_general(
            left_unit, ubuf[slot], (((1,), (1,)), ((), ())), preferred_element_type=F32
        )
        tiles[tile] = jnp.exp(sharpness * cosine).astype(BF16)

    def self_tile():
        cosine = lax.dot_general(
            ubuf[OWN], ubuf[OWN], (((1,), (1,)), ((), ())), preferred_element_type=F32
        )
        tiles[T_OWN] = jnp.where(diagonal(), 0.0, jnp.exp(sharpness * cosine)).astype(BF16)

    def product(tile, slot, j):
        return jnp.dot(tiles[tile], lbuf[slot, j], preferred_element_type=F32)

    def send_part(psend, precv, kind, j):
        copy(
            psend.at[j], precv.at[j], ssem.at[S_PART0 + kind, 0], prsem.at[kind, j], sibling
        ).start()

    def wait_part(precv, kind, j):
        copy(
            precv.at[j], precv.at[j], ssem.at[S_PART0 + kind, 0], prsem.at[kind, j], sibling
        ).wait_recv()

    def row_factor():
        total = jnp.zeros((ROWS, 1), F32)
        for j in range(LN):
            summed = acc[j]
            total = total + jnp.sum(summed * summed, axis=-1, keepdims=True)
        return keep_share * lax.rsqrt(total / CLASSES + 1e-06) * valid

    def diagonal():
        a = lax.broadcasted_iota(jnp.int32, (ROWS, ROWS), 0)
        return a == lax.broadcasted_iota(jnp.int32, (ROWS, ROWS), 1)

    def share_factor():
        row = jnp.sum(jnp.where(diagonal(), row_factor(), 0.0), axis=0, keepdims=True)
        norm[OWN] = jnp.broadcast_to(row, (8, ROWS))
        send_own(send_norm, 0)

    def finish():
        factor = row_factor()
        for j in range(LN):
            seed = lbuf[OWN, j].astype(F32)
            mixed = acc[j] * factor + (1.0 - keep_share) * seed
            out_ref[:, j * LANE : (j + 1) * LANE] = mixed.astype(BF16)

    def send_sum(q):
        lbuf[OWN, LN + q] = acc[q].astype(BF16)
        send_own(send_l, LN + q)

    def scale(tile, slot):
        tiles[tile] = (tiles[tile].astype(F32) * norm[slot, 0:1]).astype(BF16)

    @pl.when(inner)
    def _():
        def aside_rows(i):
            return asideu.at[pl.ds(pl.multiple_of(i * UROWS, UROWS), UROWS)]

        def onward_u(i):
            copy(
                aside_rows(i), aside_rows(i), ssem.at[S_ASIDE, 0], asideusem.at[i], sibling
            ).wait_recv()
            copy(
                aside_rows(i), rows(served_slot, i), ssem.at[S_ONWARD, 1],
                urecv.at[served_slot, i], served,
            ).start()

        def unit_step(i, _):
            relay_outer(send_u, wait_u, i)
            relay_inner(send_u, wait_u, i)

            @pl.when(edge)
            def _():
                copy(
                    rows(INNER2, i), aside_rows(i), ssem.at[S_ASIDE, 0], asideusem.at[i], beside
                ).start()

            @pl.when((i >= 2) & jnp.logical_not(edge))
            def _():
                onward_u(i - 2)

            copy(
                rows(OUTER, i), sibu.at[1, pl.ds(pl.multiple_of(i * UROWS, UROWS), UROWS)],
                ssem.at[S_SIB_OUTER, 0], sibrecv.at[1 + i], sibling,
            ).start()

            @pl.when(i < UN - 2)
            def _():
                send_own(send_u, i + 2)

            @pl.when(i >= UN - 2)
            def _():
                send_own(send_l, i - (UN - 2))

            @pl.when(i > 0)
            def _():
                relay_second(send_u, wait_u, i - 1)

            @pl.when(i == 2)
            def _():
                self_tile()
                wait_sib_u()
                affinity(T_SIB, sibu[0], OWN)

        lax.fori_loop(0, UN, unit_step, None)
        relay_second(send_u, wait_u, UN - 1)

        def tiles_0():
            for i in range(UN):
                copy(
                    rows(OUTER, i), sibu.at[1, pl.ds(i * UROWS, UROWS)], ssem.at[S_SIB_OUTER, 0],
                    sibrecv.at[1 + i], sibling,
                ).wait_recv()
            affinity(T_OUT, ubuf[OUTER], OWN)
            affinity(T_OUTSIB, sibu[1], OWN)
            affinity(T_OWN + 1, ubuf[OWN], OUTER)
            affinity(T_SIB + 1, sibu[0], OUTER)

        def tiles_1():
            affinity(T_OWN + 2, ubuf[OWN], INNER2)
            affinity(T_SIB + 2, sibu[0], INNER2)
            affinity(T_OUT + 1, ubuf[OUTER], INNER2)
            affinity(T_OWN + 3, ubuf[OWN], OUTER2)
            for slot in (INNER3, OUTER3):
                for i in range(UN):
                    wait_u(slot, i)

        def tiles_2():
            affinity(T_SIB + 3, sibu[0], sib_slot)
            affinity(T_OUT + 2, ubuf[OUTER], INNER3)
            affinity(T_OWN + 4, ubuf[OWN], OUTER3)
            affinity(T_OUT + 3, ubuf[OUTER], OUTER3)
            affinity(T_OUTSIB + 1, sibu[1], OUTER3)
            affinity(T_OUTSIB + 2, sibu[1], outsib_slot)

        def tiles_3():
            for slot in (NEXT, PREV):
                for i in range(UN):
                    wait_u(slot, i)
            affinity(T_OWN + 5, ubuf[OWN], NEXT)
            affinity(T_OWN + 6, ubuf[OWN], PREV)

        def scale_near():
            for i, slot in ((0, OWN), (1, OUTER), (2, INNER2)):
                scale(T_OWN + i, slot)
                scale(T_SIB + i, slot)
            scale(T_OUT, OWN)
            scale(T_OUT + 1, INNER2)
            scale(T_OUTSIB, OWN)

        def scale_far():
            scale(T_OWN + 3, OUTER2)
            scale(T_OWN + 4, OUTER3)
            scale(T_SIB + 3, sib_slot)
            scale(T_OUT + 2, INNER3)
            scale(T_OUT + 3, OUTER3)
            scale(T_OUTSIB + 1, OUTER3)
            scale(T_OUTSIB + 2, outsib_slot)
            scale(T_OWN + 5, NEXT)
            scale(T_OWN + 6, PREV)

        def combine(q, j):
            wait_part(precv1, 1, j)
            ssend[j] = (acco[q] + precv1[j]).astype(BF16)

            copy(ssend.at[j], srecv.at[j], ssem.at[S_SUM, 0], srsem.at[j], behind).start()
            wait_part(precv0, 0, j)
            acc[q] += precv0[j]

        def onward(j):
            copy(
                aside.at[j], aside.at[j], ssem.at[S_ASIDE, 0], asidesem.at[j], sibling
            ).wait_recv()
            copy(
                aside.at[j], lbuf.at[served_slot, j], ssem.at[S_ONWARD, 0],
                lrecv.at[served_slot, j], served,
            ).start()

        def grouped(q, j):
            wait_l(NEXT, j)
            wait_l(PREV, j)
            acc[q] += product(T_OWN + 5, NEXT, j) + product(T_OWN + 6, PREV, j)

        def compute(j, _):
            second = j // LN
            q = j - second * LN
            kept = jnp.where(second == 0, 0.0, 1.0 - keep_share)
            wait_l(INNER3, j)
            wait_l(OUTER3, j)
            psend1[j] = (
                product(T_OUTSIB, OWN, j)
                + product(T_OUTSIB + 1, OUTER3, j)
                + product(T_OUTSIB + 2, outsib_slot, j)
            )
            send_part(psend1, precv1, 1, j)
            psend0[j] = (
                product(T_SIB, OWN, j)
                + product(T_SIB + 1, OUTER, j)
                + product(T_SIB + 2, INNER2, j)
                + product(T_SIB + 3, sib_slot, j)
            )
            send_part(psend0, precv0, 0, j)
            acco[q] = (
                product(T_OUT, OWN, j)
                + product(T_OUT + 1, INNER2, j)
                + product(T_OUT + 2, INNER3, j)
                + product(T_OUT + 3, OUTER3, j)
            )
            acc[q] = acc[q] * kept + (
                product(T_OWN, OWN, j)
                + product(T_OWN + 1, OUTER, j)
                + product(T_OWN + 2, INNER2, j)
                + product(T_OWN + 3, OUTER2, j)
                + product(T_OWN + 4, OUTER3, j)
            )
            @pl.when(q > 0)
            def _():
                combine(q - 1, j - 1)

            @pl.when(q == LN - 1)
            def _():
                combine(q, j)

            @pl.when(q > 1)
            def _():
                grouped(q - 2, j - 2)

        def done(n):
            one = jnp.where(n >= 4, n - 1, jnp.where(n == 3, 1, 0))
            return jnp.where(n < 9, one, jnp.clip(7 + 2 * (n - 11), 7, 14))

        def step(n, _):
            @pl.when(n < 2 * LN)
            def _():
                relay_outer(send_l, wait_l, n)

            @pl.when(n < LN - 2)
            def _():
                send_own(send_l, n + 2)

            @pl.when((n >= LN - 2) & (n < 2 * LN - 2))
            def _():
                send_sum(n - (LN - 2))

            @pl.when(n < 2 * LN)
            def _():
                relay_inner(send_l, wait_l, n)

                @pl.when(n >= DETOUR)
                def _():
                    wrap_inner(send_l, n)

                @pl.when(edge & (n < DETOUR))
                def _():
                    copy(
                        lbuf.at[INNER2, n], aside.at[n], ssem.at[S_ASIDE, 1], asidesem.at[n],
                        beside,
                    ).start()

            @pl.when((n > 0) & (n <= 2 * LN))
            def _():
                relay_second(send_l, wait_l, n - 1)

            late = n - 2

            @pl.when((n < 2) & jnp.logical_not(edge))
            def _():
                onward_u(UN - 2 + n)

            @pl.when((n >= 2) & (late < DETOUR) & jnp.logical_not(edge))
            def _():
                onward(late)

            pl.when(n == 0)(tiles_0)
            pl.when(n == 1)(tiles_1)
            pl.when(n == 2)(tiles_2)
            pl.when(n == 3)(tiles_3)

            @pl.when(n == NORM_STEP)
            def _():
                relay_outer(send_norm, wait_norm, 0)
                relay_inner(send_norm, wait_norm, 0)
                wrap_inner(send_norm, 0)

            @pl.when(n == NORM_STEP + 1)
            def _():
                relay_second(send_norm, wait_norm, 0)
                scale_near()

            @pl.when(n == NORM_STEP + 2)
            def _():
                for slot in (INNER3, OUTER3, NEXT, PREV):
                    wait_norm(slot, 0)
                scale_far()

            lax.fori_loop(jnp.where(n == 0, 0, done(n - 1)), done(n), compute, None)

            @pl.when(n == LN + 1)
            def _():
                grouped(LN - 2, LN - 2)
                grouped(LN - 1, LN - 1)
                share_factor()

        lax.fori_loop(0, 2 * LN + 2, step, None)
        grouped(LN - 2, 2 * LN - 2)
        grouped(LN - 1, 2 * LN - 1)

    @pl.when(jnp.logical_not(inner))
    def _():
        def unit_step(i, _):
            send_own(send_u, i)

        lax.fori_loop(2, UN, unit_step, None)

        def label_step(j, _):
            send_own(send_l, j)

        lax.fori_loop(0, LN, label_step, None)
        self_tile()
        wait_sib_u()
        affinity(T_SIB, sibu[0], OWN)
        for slot in (NEXT, PREV):
            for i in range(UN):
                wait_u(slot, i)
        affinity(T_OWN + 5, ubuf[OWN], NEXT)
        affinity(T_OWN + 6, ubuf[OWN], PREV)

        def near(j, _):
            second = j // LN
            q = j - second * LN
            psend0[j] = product(T_SIB, OWN, j)
            send_part(psend0, precv0, 0, j)
            kept = jnp.where(second == 0, 0.0, 1.0 - keep_share)
            acc[q] = acc[q] * kept + product(T_OWN, OWN, j)

        def far(j, _):
            q = j - (j // LN) * LN
            wait_part(precv0, 0, j)
            wait_l(NEXT, j)
            wait_l(PREV, j)
            grouped = product(T_OWN + 5, NEXT, j) + product(T_OWN + 6, PREV, j)
            copy(srecv.at[j], srecv.at[j], ssem.at[S_SUM, 0], srsem.at[j], ahead).wait_recv()
            acc[q] += precv0[j] + grouped + srecv[j].astype(F32)
            pl.when(j < LN)(lambda: send_sum(q))

        lax.fori_loop(0, LN, near, None)
        lax.fori_loop(0, LN, far, None)
        share_factor()
        scale(T_OWN, OWN)
        scale(T_SIB, OWN)
        lax.fori_loop(LN, 2 * LN, near, None)
        wait_norm(NEXT, 0)
        wait_norm(PREV, 0)
        scale(T_OWN + 5, NEXT)
        scale(T_OWN + 6, PREV)
        lax.fori_loop(LN, 2 * LN, far, None)

    finish()

    def sent(slot, stream):
        copy(
            ubuf.at[slot], ubuf.at[slot], ssem.at[stream, 0], urecv.at[slot, 0], sibling
        ).wait_send()
        copy(
            lbuf.at[slot], lbuf.at[slot], ssem.at[stream, 1], lrecv.at[slot, 0], sibling
        ).wait_send()
        copy(norm.at[slot], norm.at[slot], ssem.at[stream, 2], normrecv.at[slot], sibling).wait_send()

    sent(OWN, S_OWN)
    pl.when(y < 3)(lambda: sent(OWN, S_UP))
    pl.when(y > 0)(lambda: sent(OWN, S_DOWN))
    copy(ubuf.at[OWN], sibu.at[0], ssem.at[S_SIB_OWN, 0], sibrecv.at[0], sibling).wait_send()
    copy(psend0, precv0, ssem.at[S_PART0, 0], prsem.at[0, 0], sibling).wait_send()

    @pl.when(inner)
    def _():
        sent(OUTER, S_OUTER)
        sent(INNER2, S_INNER2)
        sent(OUTER2, S_OUTER2)
        copy(ubuf.at[OUTER], sibu.at[1], ssem.at[S_SIB_OUTER, 0], sibrecv.at[1], sibling).wait_send()
        copy(psend1, precv1, ssem.at[S_PART1, 0], prsem.at[1, 0], sibling).wait_send()

    @pl.when(inner)
    def _():
        copy(ssend, srecv, ssem.at[S_SUM, 0], srsem.at[0], behind).wait_send()

    @pl.when(inner & jnp.logical_not(edge))
    def _():
        some = aside.at[pl.ds(0, DETOUR)]
        copy(some, some, ssem.at[S_ONWARD, 0], asidesem.at[0], sibling).wait_send()
        copy(asideu, asideu, ssem.at[S_ONWARD, 1], asideusem.at[0], sibling).wait_send()

    @pl.when(edge & inner)
    def _():
        sent(OUTER2, S_WRAP_O)
        block = ubuf.at[INNER2]
        copy(block, block, ssem.at[S_ASIDE, 0], urecv.at[INNER2, 0], sibling).wait_send()
        some = lbuf.at[INNER2, pl.ds(0, 2 * LN - DETOUR)]
        copy(some, some, ssem.at[S_WRAP_I, 1], lrecv.at[INNER2, 0], sibling).wait_send()
        row = norm.at[INNER2]
        copy(row, row, ssem.at[S_WRAP_I, 2], normrecv.at[INNER2], sibling).wait_send()
        some = lbuf.at[INNER2, pl.ds(0, DETOUR)]
        copy(some, some, ssem.at[S_ASIDE, 1], lrecv.at[INNER2, 0], sibling).wait_send()


def body(embeddings, labels, cluster_rows):
    vmem = pl.BlockSpec(memory_space=pltpu.VMEM)
    part = pltpu.VMEM((2 * LN, ROWS, LANE), F32)
    half = pltpu.VMEM((2 * LN, ROWS, LANE), BF16)
    return pl.pallas_call(
        kernel,
        out_shape=jax.ShapeDtypeStruct((ROWS, CLASSES), BF16),
        in_specs=[pl.BlockSpec(memory_space=pltpu.SMEM), vmem, vmem],
        out_specs=vmem,
        scratch_shapes=[
            pltpu.VMEM((SLOTS, ROWS, WIDTH), BF16),
            pltpu.VMEM((SLOTS, 2 * LN, ROWS, LANE), BF16),
            pltpu.VMEM((2, ROWS, WIDTH), BF16),
            pltpu.VMEM((N_TILES, ROWS, ROWS), BF16),
            pltpu.VMEM((LN, ROWS, LANE), F32),
            pltpu.VMEM((LN, ROWS, LANE), F32),
            part, part, part, part, half, half, half,
            pltpu.VMEM((ROWS, WIDTH), BF16),
            pltpu.VMEM((SLOTS, 8, ROWS), F32),
            pltpu.SemaphoreType.DMA((15, 3)),
            pltpu.SemaphoreType.DMA((SLOTS, UN)),
            pltpu.SemaphoreType.DMA((SLOTS, 2 * LN)),
            pltpu.SemaphoreType.DMA((1 + UN,)),
            pltpu.SemaphoreType.DMA((2, 2 * LN)),
            pltpu.SemaphoreType.DMA((2 * LN,)),
            pltpu.SemaphoreType.DMA((2 * LN,)),
            pltpu.SemaphoreType.DMA((UN,)),
            pltpu.SemaphoreType.DMA((SLOTS,)),
        ],
        compiler_params=pltpu.CompilerParams(
            collective_id=0, has_side_effects=True, vmem_limit_bytes=60 * 2**20
        ),
        cost_estimate=pl.CostEstimate(
            flops=14 * 10**9, bytes_accessed=2 * 10**6, transcendentals=3 * 10**6
        ),
    )(cluster_rows, embeddings, labels)


def solution(mesh):
    placed = (P(("grp", "dev"), None), P(("grp", "dev"), None), P(("grp", "dev")))
    return jax.shard_map(
        body, mesh=mesh, in_specs=placed, out_specs=P(("grp", "dev"), None), check_vma=False
    )
```

```python
import functools
import math

import jax
import jax.numpy as jnp
from jax import lax
from jax.experimental import pallas as pl
from jax.experimental.pallas import tpu as pltpu
from jax.sharding import PartitionSpec as P

MESH = pl.DeviceIdType.MESH
F32 = jnp.float32
BF16 = jnp.bfloat16

sharpness = 25.0
keep_share = 0.8

ROWS = 384
WIDTH = 768
CLASSES = 896
LANE = 128
UN = 6
UROWS = ROWS // UN
LN = CLASSES // LANE

OWN, OUTER, INNER2, OUTER2, INNER3, OUTER3, NEXT, PREV = range(8)
SLOTS = 8

(S_OWN, S_UP, S_DOWN, S_OUTER, S_INNER2, S_OUTER2, S_WRAP_I, S_WRAP_O, S_SIB_OWN, S_SIB_OUTER, S_PART0, S_PART1,
 S_SUM, S_ASIDE, S_ONWARD) = range(15)
NORM_STEP = 9
DETOUR = 13

T_OWN, T_SIB, T_OUT, T_OUTSIB = 0, 7, 11, 15
N_TILES = 18
OWN_SOURCES = (OWN, OUTER, INNER2, OUTER2, OUTER3, NEXT, PREV)
SIB_SOURCES = (OWN, OUTER, INNER2, None)
OUT_SOURCES = (OWN, INNER2, INNER3, OUTER3)
OUTSIB_SOURCES = (OWN, OUTER3, None)


def kernel(
    count_ref, emb_ref, lab_ref, out_ref,
    ubuf, lbuf, sibu, tiles, acc, acco, psend0, psend1, precv0, precv1, ssend, srecv, aside, asideu, norm,
    ssem, urecv, lrecv, sibrecv, prsem, srsem, asidesem, asideusem, normrecv,
):
    g, d = lax.axis_index("grp"), lax.axis_index("dev")
    x, k, c = d // 8, (d // 2) % 4, d % 2
    z, y = (g // 4) * 4 + k, g % 4
    s = 1 - 2 * (k // 2)
    inner = (k == 1) | (k == 2)
    edge = (y == 0) | (y == 3)

    def at(x, y, z, c):
        x, y, z = (x + 4) % 4, (y + 4) % 4, (z + 16) % 8
        return ((z // 4) * 4 + y, x * 8 + (z % 4) * 2 + c)

    sibling = at(x, y, z, 1 - c)
    ahead = at(x, y, z + s, c)
    behind = at(x, y, z - s, c)
    up, down = at(x, y + 1, z, c), at(x, y - 1, z, c)
    right, left = at(x + s, y, z, c), at(x - s, y, z, c)
    wrap_i = at(x, 3 - y, z + s + 4, c)
    wrap_o = at(x, 3 - y, z + 2 * s + 4, c)
    wrap_slot = NEXT + y // 3
    relay = at(x, 3 - y, z + 4 + s * (2 - ((k == 1) | (k == 2)).astype(jnp.int32)), c)
    side = (c + k // 2) % 2
    sib_slot = OUTER2 + 2 * side
    outsib_slot = INNER2 + 2 * side

    beside = at(x, 1 + y // 3, z, c)
    served = at(x, 3 - 3 * (y // 2), z + s + 4, c)
    served_slot = NEXT + y // 2
    server = at(x, 1 + (3 - y) // 3, z + s + 4, c)

    barrier = pltpu.get_barrier_semaphore()

    def greet(device):
        pl.semaphore_signal(barrier, inc=1, device_id=device, device_id_type=MESH)

    for device in (sibling, ahead, behind, up, down, right, left):
        greet(device)

    @pl.when(edge)
    def _():
        greet(relay)

    @pl.when(edge & inner)
    def _():
        greet(wrap_i)
        greet(wrap_o)
        greet(server)

    @pl.when(jnp.logical_not(edge) & inner)
    def _():
        greet(served)

    def copy(src, dst, send_sem, recv_sem, device):
        return pltpu.make_async_remote_copy(
            src_ref=src, dst_ref=dst, send_sem=send_sem, recv_sem=recv_sem, device_id=device,
            device_id_type=MESH,
        )

    def rows(slot, i):
        return ubuf.at[slot, pl.ds(pl.multiple_of(i * UROWS, UROWS), UROWS)]

    def send_u(src_slot, dst_slot, i, stream, device):
        copy(
            rows(src_slot, i), rows(dst_slot, i), ssem.at[stream, 0], urecv.at[dst_slot, i], device
        ).start()

    def send_l(src_slot, dst_slot, j, stream, device):
        copy(
            lbuf.at[src_slot, j], lbuf.at[dst_slot, j], ssem.at[stream, 1], lrecv.at[dst_slot, j],
            device,
        ).start()

    def wait_u(slot, i):
        copy(rows(slot, i), rows(slot, i), ssem.at[S_OWN, 0], urecv.at[slot, i], sibling).wait_recv()

    def wait_l(slot, j):
        copy(
            lbuf.at[slot, j], lbuf.at[slot, j], ssem.at[S_OWN, 1], lrecv.at[slot, j], sibling
        ).wait_recv()

    def send_norm(src_slot, dst_slot, _, stream, device):
        copy(
            norm.at[src_slot], norm.at[dst_slot], ssem.at[stream, 2], normrecv.at[dst_slot], device
        ).start()

    def wait_norm(slot, _):
        copy(
            norm.at[slot], norm.at[slot], ssem.at[S_OWN, 2], normrecv.at[slot], sibling
        ).wait_recv()

    own_slot = INNER2 - (1 - ((k == 1) | (k == 2)).astype(jnp.int32))

    def send_own(send, i):
        send(OWN, own_slot, i, S_OWN, ahead)

        @pl.when(y < 3)
        def _():
            send(OWN, PREV, i, S_UP, up)

        @pl.when(y > 0)
        def _():
            send(OWN, NEXT, i, S_DOWN, down)

    def relay_outer(send, wait, i):
        wait(OUTER, i)
        send(OUTER, OUTER2, i, S_OUTER, ahead)

    def relay_inner(send, wait, i):
        wait(INNER2, i)
        send(INNER2, INNER3, i, S_INNER2, right)

    def wrap_inner(send, i):
        @pl.when(edge)
        def _():
            send(INNER2, wrap_slot, i, S_WRAP_I, wrap_i)

    def relay_second(send, wait, i):
        wait(OUTER2, i)
        send(OUTER2, OUTER3, i, S_OUTER2, right)

        @pl.when(edge)
        def _():
            send(OUTER2, wrap_slot, i, S_WRAP_O, wrap_o)

    acc[...] = jnp.zeros_like(acc)
    valid = (lax.broadcasted_iota(jnp.int32, (ROWS, 1), 0) < count_ref[0]).astype(F32)

    values = emb_ref[...].astype(F32)
    scaled = values * lax.rsqrt(jnp.mean(values * values, axis=-1, keepdims=True) + 1e-06)
    ubuf[OWN] = (scaled / math.sqrt(WIDTH)).astype(BF16)
    pl.semaphore_wait(
        barrier, 7 + jnp.where(inner, jnp.where(edge, 4, 1), jnp.where(edge, 1, 0))
    )
    copy(ubuf.at[OWN], sibu.at[0], ssem.at[S_SIB_OWN, 0], sibrecv.at[0], sibling).start()
    for i in range(2):
        send_own(send_u, i)
    for j in range(LN):
        lbuf[OWN, j] = (lab_ref[:, j * LANE : (j + 1) * LANE].astype(F32) * valid).astype(BF16)

    def wait_sib_u():
        copy(ubuf.at[OWN], sibu.at[0], ssem.at[S_SIB_OWN, 0], sibrecv.at[0], sibling).wait_recv()

    def affinity(tile, left_unit, slot):
        cosine = lax.dot_general(
            left_unit, ubuf[slot], (((1,), (1,)), ((), ())), preferred_element_type=F32
        )
        tiles[tile] = jnp.exp(sharpness * cosine).astype(BF16)

    def self_tile():
        cosine = lax.dot_general(
            ubuf[OWN], ubuf[OWN], (((1,), (1,)), ((), ())), preferred_element_type=F32
        )
        tiles[T_OWN] = jnp.where(diagonal(), 0.0, jnp.exp(sharpness * cosine)).astype(BF16)

    def product(tile, slot, j):
        return jnp.dot(tiles[tile], lbuf[slot, j], preferred_element_type=F32)

    def send_part(psend, precv, kind, j):
        copy(
            psend.at[j], precv.at[j], ssem.at[S_PART0 + kind, 0], prsem.at[kind, j], sibling
        ).start()

    def wait_part(precv, kind, j):
        copy(
            precv.at[j], precv.at[j], ssem.at[S_PART0 + kind, 0], prsem.at[kind, j], sibling
        ).wait_recv()

    def row_factor():
        total = jnp.zeros((ROWS, 1), F32)
        for j in range(LN):
            summed = acc[j]
            total = total + jnp.sum(summed * summed, axis=-1, keepdims=True)
        return keep_share * lax.rsqrt(total / CLASSES + 1e-06) * valid

    def diagonal():
        a = lax.broadcasted_iota(jnp.int32, (ROWS, ROWS), 0)
        return a == lax.broadcasted_iota(jnp.int32, (ROWS, ROWS), 1)

    def share_factor():
        row = jnp.sum(jnp.where(diagonal(), row_factor(), 0.0), axis=0, keepdims=True)
        norm[OWN] = jnp.broadcast_to(row, (8, ROWS))
        send_own(send_norm, 0)

    def finish():
        factor = row_factor()
        for j in range(LN):
            seed = lbuf[OWN, j].astype(F32)
            mixed = acc[j] * factor + (1.0 - keep_share) * seed
            out_ref[:, j * LANE : (j + 1) * LANE] = mixed.astype(BF16)

    def send_sum(q):
        lbuf[OWN, LN + q] = acc[q].astype(BF16)
        send_own(send_l, LN + q)

    def scale(tile, slot):
        tiles[tile] = (tiles[tile].astype(F32) * norm[slot, 0:1]).astype(BF16)

    @pl.when(inner)
    def _():
        def aside_rows(i):
            return asideu.at[pl.ds(pl.multiple_of(i * UROWS, UROWS), UROWS)]

        def onward_u(i):
            copy(
                aside_rows(i), aside_rows(i), ssem.at[S_ASIDE, 0], asideusem.at[i], sibling
            ).wait_recv()
            copy(
                aside_rows(i), rows(served_slot, i), ssem.at[S_ONWARD, 1],
                urecv.at[served_slot, i], served,
            ).start()

        def unit_step(i, _):
            relay_outer(send_u, wait_u, i)
            relay_inner(send_u, wait_u, i)

            @pl.when(edge)
            def _():
                copy(
                    rows(INNER2, i), aside_rows(i), ssem.at[S_ASIDE, 0], asideusem.at[i], beside
                ).start()

            @pl.when((i >= 2) & jnp.logical_not(edge))
            def _():
                onward_u(i - 2)

            copy(
                rows(OUTER, i), sibu.at[1, pl.ds(pl.multiple_of(i * UROWS, UROWS), UROWS)],
                ssem.at[S_SIB_OUTER, 0], sibrecv.at[1 + i], sibling,
            ).start()

            @pl.when(i < UN - 2)
            def _():
                send_own(send_u, i + 2)

            @pl.when(i >= UN - 2)
            def _():
                send_own(send_l, i - (UN - 2))

            @pl.when(i > 0)
            def _():
                relay_second(send_u, wait_u, i - 1)

            @pl.when(i == 2)
            def _():
                self_tile()
                wait_sib_u()
                affinity(T_SIB, sibu[0], OWN)

        lax.fori_loop(0, UN, unit_step, None)
        relay_second(send_u, wait_u, UN - 1)

        def tiles_0():
            for i in range(UN):
                copy(
                    rows(OUTER, i), sibu.at[1, pl.ds(i * UROWS, UROWS)], ssem.at[S_SIB_OUTER, 0],
                    sibrecv.at[1 + i], sibling,
                ).wait_recv()
            affinity(T_OUT, ubuf[OUTER], OWN)
            affinity(T_OUTSIB, sibu[1], OWN)
            affinity(T_OWN + 1, ubuf[OWN], OUTER)
            affinity(T_SIB + 1, sibu[0], OUTER)

        def tiles_1():
            affinity(T_OWN + 2, ubuf[OWN], INNER2)
            affinity(T_SIB + 2, sibu[0], INNER2)
            affinity(T_OUT + 1, ubuf[OUTER], INNER2)
            affinity(T_OWN + 3, ubuf[OWN], OUTER2)
            for slot in (INNER3, OUTER3):
                for i in range(UN):
                    wait_u(slot, i)

        def tiles_2():
            affinity(T_SIB + 3, sibu[0], sib_slot)
            affinity(T_OUT + 2, ubuf[OUTER], INNER3)
            affinity(T_OWN + 4, ubuf[OWN], OUTER3)
            affinity(T_OUT + 3, ubuf[OUTER], OUTER3)
            affinity(T_OUTSIB + 1, sibu[1], OUTER3)
            affinity(T_OUTSIB + 2, sibu[1], outsib_slot)

        def tiles_3():
            for slot in (NEXT, PREV):
                for i in range(UN):
                    wait_u(slot, i)
            affinity(T_OWN + 5, ubuf[OWN], NEXT)
            affinity(T_OWN + 6, ubuf[OWN], PREV)

        def scale_near():
            for i, slot in ((0, OWN), (1, OUTER), (2, INNER2)):
                scale(T_OWN + i, slot)
                scale(T_SIB + i, slot)
            scale(T_OUT, OWN)
            scale(T_OUT + 1, INNER2)
            scale(T_OUTSIB, OWN)

        def scale_far():
            scale(T_OWN + 3, OUTER2)
            scale(T_OWN + 4, OUTER3)
            scale(T_SIB + 3, sib_slot)
            scale(T_OUT + 2, INNER3)
            scale(T_OUT + 3, OUTER3)
            scale(T_OUTSIB + 1, OUTER3)
            scale(T_OUTSIB + 2, outsib_slot)
            scale(T_OWN + 5, NEXT)
            scale(T_OWN + 6, PREV)

        def combine(q, j):
            wait_part(precv1, 1, j)
            ssend[j] = (acco[q] + precv1[j].astype(F32)).astype(BF16)

            copy(ssend.at[j], srecv.at[j], ssem.at[S_SUM, 0], srsem.at[j], behind).start()
            wait_part(precv0, 0, j)
            acc[q] += precv0[j].astype(F32)

        def onward(j):
            copy(
                aside.at[j], aside.at[j], ssem.at[S_ASIDE, 0], asidesem.at[j], sibling
            ).wait_recv()
            copy(
                aside.at[j], lbuf.at[served_slot, j], ssem.at[S_ONWARD, 0],
                lrecv.at[served_slot, j], served,
            ).start()

        def grouped(q, j):
            wait_l(NEXT, j)
            wait_l(PREV, j)
            acc[q] += product(T_OWN + 5, NEXT, j) + product(T_OWN + 6, PREV, j)

        def compute(j, _):
            second = j // LN
            q = j - second * LN
            kept = jnp.where(second == 0, 0.0, 1.0 - keep_share)
            wait_l(INNER3, j)
            wait_l(OUTER3, j)
            psend1[j] = (
                product(T_OUTSIB, OWN, j)
                + product(T_OUTSIB + 1, OUTER3, j)
                + product(T_OUTSIB + 2, outsib_slot, j)
            ).astype(BF16)
            send_part(psend1, precv1, 1, j)
            psend0[j] = (
                product(T_SIB, OWN, j)
                + product(T_SIB + 1, OUTER, j)
                + product(T_SIB + 2, INNER2, j)
                + product(T_SIB + 3, sib_slot, j)
            ).astype(BF16)
            send_part(psend0, precv0, 0, j)
            acco[q] = (
                product(T_OUT, OWN, j)
                + product(T_OUT + 1, INNER2, j)
                + product(T_OUT + 2, INNER3, j)
                + product(T_OUT + 3, OUTER3, j)
            )
            acc[q] = acc[q] * kept + (
                product(T_OWN, OWN, j)
                + product(T_OWN + 1, OUTER, j)
                + product(T_OWN + 2, INNER2, j)
                + product(T_OWN + 3, OUTER2, j)
                + product(T_OWN + 4, OUTER3, j)
            )
            @pl.when(q > 0)
            def _():
                combine(q - 1, j - 1)

            @pl.when(q == LN - 1)
            def _():
                combine(q, j)

            @pl.when(q > 1)
            def _():
                grouped(q - 2, j - 2)

        def done(n):
            one = jnp.where(n >= 4, n - 1, jnp.where(n == 3, 1, 0))
            return jnp.where(n < 9, one, jnp.clip(7 + 2 * (n - 11), 7, 14))

        def step(n, _):
            @pl.when(n < 2 * LN)
            def _():
                relay_outer(send_l, wait_l, n)

            @pl.when(n < LN - 2)
            def _():
                send_own(send_l, n + 2)

            @pl.when((n >= LN - 2) & (n < 2 * LN - 2))
            def _():
                send_sum(n - (LN - 2))

            @pl.when(n < 2 * LN)
            def _():
                relay_inner(send_l, wait_l, n)

                @pl.when(n >= DETOUR)
                def _():
                    wrap_inner(send_l, n)

                @pl.when(edge & (n < DETOUR))
                def _():
                    copy(
                        lbuf.at[INNER2, n], aside.at[n], ssem.at[S_ASIDE, 1], asidesem.at[n],
                        beside,
                    ).start()

            @pl.when((n > 0) & (n <= 2 * LN))
            def _():
                relay_second(send_l, wait_l, n - 1)

            late = n - 2

            @pl.when((n < 2) & jnp.logical_not(edge))
            def _():
                onward_u(UN - 2 + n)

            @pl.when((n >= 2) & (late < DETOUR) & jnp.logical_not(edge))
            def _():
                onward(late)

            pl.when(n == 0)(tiles_0)
            pl.when(n == 1)(tiles_1)
            pl.when(n == 2)(tiles_2)
            pl.when(n == 3)(tiles_3)

            @pl.when(n == NORM_STEP)
            def _():
                relay_outer(send_norm, wait_norm, 0)
                relay_inner(send_norm, wait_norm, 0)
                wrap_inner(send_norm, 0)

            @pl.when(n == NORM_STEP + 1)
            def _():
                relay_second(send_norm, wait_norm, 0)
                scale_near()

            @pl.when(n == NORM_STEP + 2)
            def _():
                for slot in (INNER3, OUTER3, NEXT, PREV):
                    wait_norm(slot, 0)
                scale_far()

            lax.fori_loop(jnp.where(n == 0, 0, done(n - 1)), done(n), compute, None)

            @pl.when(n == LN + 1)
            def _():
                grouped(LN - 2, LN - 2)
                grouped(LN - 1, LN - 1)
                share_factor()

        lax.fori_loop(0, 2 * LN + 2, step, None)
        grouped(LN - 2, 2 * LN - 2)
        grouped(LN - 1, 2 * LN - 1)

    @pl.when(jnp.logical_not(inner))
    def _():
        def unit_step(i, _):
            send_own(send_u, i)

        lax.fori_loop(2, UN, unit_step, None)

        def label_step(j, _):
            send_own(send_l, j)

        lax.fori_loop(0, LN, label_step, None)
        self_tile()
        wait_sib_u()
        affinity(T_SIB, sibu[0], OWN)
        for slot in (NEXT, PREV):
            for i in range(UN):
                wait_u(slot, i)
        affinity(T_OWN + 5, ubuf[OWN], NEXT)
        affinity(T_OWN + 6, ubuf[OWN], PREV)

        def near(j, _):
            second = j // LN
            q = j - second * LN
            psend0[j] = product(T_SIB, OWN, j).astype(BF16)
            send_part(psend0, precv0, 0, j)
            kept = jnp.where(second == 0, 0.0, 1.0 - keep_share)
            acc[q] = acc[q] * kept + product(T_OWN, OWN, j)

        def far(j, _):
            q = j - (j // LN) * LN
            wait_part(precv0, 0, j)
            wait_l(NEXT, j)
            wait_l(PREV, j)
            grouped = product(T_OWN + 5, NEXT, j) + product(T_OWN + 6, PREV, j)
            copy(srecv.at[j], srecv.at[j], ssem.at[S_SUM, 0], srsem.at[j], ahead).wait_recv()
            acc[q] += precv0[j].astype(F32) + grouped + srecv[j].astype(F32)
            pl.when(j < LN)(lambda: send_sum(q))

        lax.fori_loop(0, LN, near, None)
        lax.fori_loop(0, LN, far, None)
        share_factor()
        scale(T_OWN, OWN)
        scale(T_SIB, OWN)
        lax.fori_loop(LN, 2 * LN, near, None)
        wait_norm(NEXT, 0)
        wait_norm(PREV, 0)
        scale(T_OWN + 5, NEXT)
        scale(T_OWN + 6, PREV)
        lax.fori_loop(LN, 2 * LN, far, None)

    finish()

    def sent(slot, stream):
        copy(
            ubuf.at[slot], ubuf.at[slot], ssem.at[stream, 0], urecv.at[slot, 0], sibling
        ).wait_send()
        copy(
            lbuf.at[slot], lbuf.at[slot], ssem.at[stream, 1], lrecv.at[slot, 0], sibling
        ).wait_send()
        copy(norm.at[slot], norm.at[slot], ssem.at[stream, 2], normrecv.at[slot], sibling).wait_send()

    sent(OWN, S_OWN)
    pl.when(y < 3)(lambda: sent(OWN, S_UP))
    pl.when(y > 0)(lambda: sent(OWN, S_DOWN))
    copy(ubuf.at[OWN], sibu.at[0], ssem.at[S_SIB_OWN, 0], sibrecv.at[0], sibling).wait_send()
    copy(psend0, precv0, ssem.at[S_PART0, 0], prsem.at[0, 0], sibling).wait_send()

    @pl.when(inner)
    def _():
        sent(OUTER, S_OUTER)
        sent(INNER2, S_INNER2)
        sent(OUTER2, S_OUTER2)
        copy(ubuf.at[OUTER], sibu.at[1], ssem.at[S_SIB_OUTER, 0], sibrecv.at[1], sibling).wait_send()
        copy(psend1, precv1, ssem.at[S_PART1, 0], prsem.at[1, 0], sibling).wait_send()

    @pl.when(inner)
    def _():
        copy(ssend, srecv, ssem.at[S_SUM, 0], srsem.at[0], behind).wait_send()

    @pl.when(inner & jnp.logical_not(edge))
    def _():
        some = aside.at[pl.ds(0, DETOUR)]
        copy(some, some, ssem.at[S_ONWARD, 0], asidesem.at[0], sibling).wait_send()
        copy(asideu, asideu, ssem.at[S_ONWARD, 1], asideusem.at[0], sibling).wait_send()

    @pl.when(edge & inner)
    def _():
        sent(OUTER2, S_WRAP_O)
        block = ubuf.at[INNER2]
        copy(block, block, ssem.at[S_ASIDE, 0], urecv.at[INNER2, 0], sibling).wait_send()
        some = lbuf.at[INNER2, pl.ds(0, 2 * LN - DETOUR)]
        copy(some, some, ssem.at[S_WRAP_I, 1], lrecv.at[INNER2, 0], sibling).wait_send()
        row = norm.at[INNER2]
        copy(row, row, ssem.at[S_WRAP_I, 2], normrecv.at[INNER2], sibling).wait_send()
        some = lbuf.at[INNER2, pl.ds(0, DETOUR)]
        copy(some, some, ssem.at[S_ASIDE, 1], lrecv.at[INNER2, 0], sibling).wait_send()


def body(embeddings, labels, cluster_rows):
    vmem = pl.BlockSpec(memory_space=pltpu.VMEM)
    part = pltpu.VMEM((2 * LN, ROWS, LANE), BF16)
    half = pltpu.VMEM((2 * LN, ROWS, LANE), BF16)
    return pl.pallas_call(
        kernel,
        out_shape=jax.ShapeDtypeStruct((ROWS, CLASSES), BF16),
        in_specs=[pl.BlockSpec(memory_space=pltpu.SMEM), vmem, vmem],
        out_specs=vmem,
        scratch_shapes=[
            pltpu.VMEM((SLOTS, ROWS, WIDTH), BF16),
            pltpu.VMEM((SLOTS, 2 * LN, ROWS, LANE), BF16),
            pltpu.VMEM((2, ROWS, WIDTH), BF16),
            pltpu.VMEM((N_TILES, ROWS, ROWS), BF16),
            pltpu.VMEM((LN, ROWS, LANE), F32),
            pltpu.VMEM((LN, ROWS, LANE), F32),
            part, part, part, part, half, half, half,
            pltpu.VMEM((ROWS, WIDTH), BF16),
            pltpu.VMEM((SLOTS, 8, ROWS), F32),
            pltpu.SemaphoreType.DMA((15, 3)),
            pltpu.SemaphoreType.DMA((SLOTS, UN)),
            pltpu.SemaphoreType.DMA((SLOTS, 2 * LN)),
            pltpu.SemaphoreType.DMA((1 + UN,)),
            pltpu.SemaphoreType.DMA((2, 2 * LN)),
            pltpu.SemaphoreType.DMA((2 * LN,)),
            pltpu.SemaphoreType.DMA((2 * LN,)),
            pltpu.SemaphoreType.DMA((UN,)),
            pltpu.SemaphoreType.DMA((SLOTS,)),
        ],
        compiler_params=pltpu.CompilerParams(
            collective_id=0, has_side_effects=True, vmem_limit_bytes=60 * 2**20
        ),
        cost_estimate=pl.CostEstimate(
            flops=14 * 10**9, bytes_accessed=2 * 10**6, transcendentals=3 * 10**6
        ),
    )(cluster_rows, embeddings, labels)


def solution(mesh):
    placed = (P(("grp", "dev"), None), P(("grp", "dev"), None), P(("grp", "dev")))
    return jax.shard_map(
        body, mesh=mesh, in_specs=placed, out_specs=P(("grp", "dev"), None), check_vma=False
    )
```
